512 devices in a mesh: tensor: 8 (over y), expert: 64 (over x, z, core).
Axes of the slice: x: 4, y: 8, z: 8, core: 2. Of those that a mesh axis runs over, the one named last changes fastest.
Arguments:
- tokens: bfloat16 [4096, 4096], P('expert', 'tensor'), may hold values from -6 to 6
- gate_weight: bfloat16 [64, 1536, 4096], P('expert', 'tensor'), may hold values from -0.09375 to 0.09375
- up_weight: bfloat16 [64, 1536, 4096], P('expert', 'tensor'), may hold values from -0.09375 to 0.09375
- down_weight: bfloat16 [64, 1536, 4096], P('expert', None, 'tensor'), may hold values from -0.15625 to 0.15625
- expert_ids: int32 [4096, 8], P('expert'), may hold values from 0 to 63, all different within a row; in each aligned block of 64 rows (0 to 63, 64 to 127, ...) at most 16 rows name the same one
- gate_probs: float32 [4096, 8], P('expert'), may hold values from 0.05 to 0.25
Outputs:
- mixed: bfloat16 [4096, 4096], P('expert', 'tensor')
The draws below stay inside these ranges and needn't reach their ends.
Inputs may be any that keep to these rules, and one draw needn't show every extreme that they name: `expert_ids`: in each aligned block of 64 rows (the tokens of one index of expert) no expert is named by more than 16 rows, a bound that some block reaches; the 8 experts of a row differ.
All inputs are finite; a program needn't handle non-finite values.
Results may differ from the reference program's by a relative error of at most 0.0057.
Values may be sent and summed in bfloat16 or wider, within the bound.
A program may use at most 64 MiB of HBM per device.

```python
import math
import jax
import jax.numpy as jnp
import numpy as np
from jax import lax

D = 4096
FF = 1536
TOP = 8
TOK_EP = 64
EXPERTS = 64
CAP = 16
TOKENS = 4096


def block_scale(rng, dims, cuts, least, top_value):
    level = 1.0
    for dim, parts in cuts:
        heights = jax.random.uniform(jax.random.fold_in(jax.random.fold_in(rng, 6), dim), (parts,), jnp.float32, least / len(cuts), top_value / len(cuts))
        level = level * jnp.repeat(jnp.exp(heights), dims[dim] // parts).reshape((-1,) + (1,) * (len(dims) - 1 - dim))
    return level


def deal_out(own_key, own, number, rows, amount, top, most, slope):
    ranking = jax.random.permutation(own_key, amount)
    packed, common = portions_of(amount, rows * top, most, slope, True), portions_of(amount, rows * top, most, slope, False)
    places = jnp.arange(amount)

    def named(lengths, turn):
        used = int((lengths > 0).sum())
        fixed = max(1, used // 4)
        shifted = fixed + (places - fixed + turn * (used - fixed)) % max(1, amount - fixed)
        return jnp.zeros((amount,), jnp.int32).at[ranking[jnp.where(places < fixed, places, shifted)]].set(jnp.asarray(lengths, jnp.int32))

    lengths = jnp.where(number % 4 == 0, named(packed, number // 4), named(common, number - number // 4 - 1))
    mixed = jax.random.permutation(jax.random.fold_in(own, 3), amount)
    giver, taker = mixed[0:amount // 2 * 2:2], mixed[1:amount // 2 * 2:2]
    margin = jnp.minimum(lengths[giver] - 1, most - lengths[taker]) // 2
    margin = jnp.where((giver == ranking[0]) | (taker == ranking[0]) | (lengths[taker] == 0), 0, jnp.maximum(margin, 0))
    shifted = jax.random.randint(jax.random.fold_in(own, 4), (amount // 2,), 0, 1 << 20) % (margin + 1)
    lengths = lengths.at[giver].add(-shifted).at[taker].add(shifted)
    labels = jnp.searchsorted(jnp.cumsum(lengths), jnp.arange(rows * top), side="right").astype(jnp.int32)
    table = labels.reshape(top, rows).T
    table = table[jax.random.permutation(jax.random.fold_in(own, 1), rows)]
    turn = jax.random.randint(jax.random.fold_in(own, 2), (rows, 1), 0, top)
    return jnp.take_along_axis(table, (jnp.arange(top)[None, :] + turn) % top, axis=1)


def portions_of(number_of, total, reach, lean, full):
    weights = [(1 << 20) // math.isqrt(standing ** lean) + 1 for standing in range(1, number_of + 1)]
    largest = reach if full else min(reach, max(-(-total // number_of), total * weights[0] // sum(weights)))
    least = 1 if total - largest >= number_of - 1 else 0
    counts, rest = [largest] + [least] * (number_of - 1), total - largest - least * (number_of - 1)
    while rest > 0:
        free = [i for i in range(1, number_of) if counts[i] < largest] or [i for i in range(1, number_of) if counts[i] < reach]
        whole, left = sum([weights[i] for i in free]), rest
        for i in free:
            addition = min(reach - counts[i], max(1, left * weights[i] // whole), rest)
            counts[i] = counts[i] + addition
            rest = rest - addition
    return np.array(counts)


def scatter_about(stream_key, extent, width, reach, cuts=(), kind=jnp.bfloat16):
    result = width * jax.random.normal(stream_key, extent, jnp.float32)
    if cuts:
        result = result * block_scale(stream_key, extent, cuts, -0.22, 0.18)
    return jnp.clip(result, -reach, reach).astype(kind)


def setup_inputs(seed: int = 0) -> dict:
    key_of = jax.random.split(jax.random.key(seed), 7)
    tokens = scatter_about(key_of[0], (TOKENS, D), 1.0, 6.0, ((0, 64), (1, 8)))
    gate_weight = scatter_about(key_of[1], (EXPERTS, FF, D), D ** -0.5, 0.09375, ((0, 64), (1, 8)))
    up_weight = scatter_about(key_of[2], (EXPERTS, FF, D), D ** -0.5, 0.09375, ((0, 64), (1, 8)))
    down_weight = scatter_about(key_of[3], (EXPERTS, FF, D), FF ** -0.5, 0.15625, ((0, 64), (2, 8)))
    expert_ids_keys = jax.random.split(jax.random.fold_in(key_of[4], 1), TOKENS // TOK_EP)
    expert_ids_turns = jax.random.permutation(jax.random.fold_in(key_of[4], 3), TOKENS // TOK_EP)
    expert_ids = jax.vmap(lambda own, number: deal_out(jax.random.fold_in(key_of[4], 2), own, number, TOK_EP, EXPERTS, TOP, CAP, 2))(expert_ids_keys, expert_ids_turns).reshape((TOKENS, TOP))
    gate_probs = jnp.clip(0.05 + 0.2 * jax.random.uniform(key_of[5], (TOKENS, TOP), jnp.float32) ** block_scale(key_of[5], (TOKENS, TOP), ((0, 64),), -0.2, 0.2), 0.05, 0.25)
    return dict(tokens=tokens, gate_weight=gate_weight, up_weight=up_weight, down_weight=down_weight, expert_ids=expert_ids, gate_probs=gate_probs)


def reference(tokens, gate_weight, up_weight, down_weight, expert_ids, gate_probs):
    groups = TOKENS // TOK_EP
    flat = expert_ids.reshape(groups, TOK_EP * TOP)
    onehot = (flat[:, :, None] == jnp.arange(EXPERTS, dtype=jnp.int32)[None, None, :]).astype(jnp.int32)
    before = jnp.cumsum(onehot, axis=1) - onehot
    slots = jnp.sum(before * onehot, axis=2).astype(jnp.int32)
    target = (flat * CAP + slots).reshape(groups, TOK_EP, TOP)
    inputs = tokens.reshape(groups, TOK_EP, D).astype(jnp.float32)
    probs = gate_probs.reshape(groups, TOK_EP, TOP).astype(jnp.float32)
    positions = jnp.arange(CAP, dtype=jnp.int32)
    contract = (((1,), (1,)), ((), ()))

    def one_expert(total, pieces):
        index, w_gate, w_up, w_down = pieces
        wanted = (index * CAP + positions).astype(jnp.int32)
        match = target[:, None, :, :] == wanted[None, :, None, None]
        pick = jnp.any(match, axis=3).astype(jnp.float32)
        buffer = jnp.einsum("gcr,grd->gcd", pick, inputs, precision=lax.Precision.HIGHEST)
        buffer = buffer.astype(jnp.bfloat16).reshape(groups * CAP, D)
        gate = lax.dot_general(buffer, w_gate, contract, preferred_element_type=jnp.float32)
        up = lax.dot_general(buffer, w_up, contract, preferred_element_type=jnp.float32)
        hidden = (jax.nn.silu(gate) * up).astype(jnp.bfloat16)
        output = jnp.dot(hidden, w_down, preferred_element_type=jnp.float32).astype(jnp.bfloat16)
        output = output.reshape(groups, CAP, D).astype(jnp.float32)
        weight = jnp.sum(match.astype(jnp.float32) * probs[:, None, :, :], axis=3)
        total = total + jnp.einsum("gcr,gcd->grd", weight, output, precision=lax.Precision.HIGHEST)
        return total, None

    start = jnp.zeros((groups, TOK_EP, D), jnp.float32)
    total, _ = lax.scan(one_expert, start, (jnp.arange(EXPERTS, dtype=jnp.int32), gate_weight, up_weight, down_weight))
    return total.reshape(TOKENS, D).astype(jnp.bfloat16)
```

```python
import functools

import jax
import jax.numpy as jnp
from jax import lax
from jax.experimental import pallas as pl
from jax.experimental.pallas import tpu as pltpu
from jax.sharding import PartitionSpec as P

MESH = pl.DeviceIdType.MESH
BF16 = jnp.bfloat16
F32 = jnp.float32
NX, NY, NZ, NC = 4, 8, 8, 2
ROW = NX * NC
ROWS = 64
SLOTS = 16
SLICE = 512
HALF = 2048
HID = 192
PIECE = HID // 2
META = 128
GROUPS = 4


def dot(a, b, da, db):
    return lax.dot_general(a, b, (((da,), (db,)), ((), ())), preferred_element_type=F32)


def kernel(
    tok, gate, up, down, ids, prob, out,
    blocks, picked, arrived, weights, down_v, own, part_out, part_in,
    hidden, outputs, returned, sums_out, sums_in, own_sum,
    pg_s, pg_r, w_s, w_r, lw, ld, z_s, z_r, x_s, x_r, p_s, p_r, h_s, h_r, o_s, o_r, f_s, f_r,
):
    t = lax.axis_index("tensor")
    e = lax.axis_index("expert")
    c = lax.rem(e, NC)
    z = lax.rem(e // NC, NZ)
    x = e // (NC * NZ)
    me = x * NC + c
    q = lax.rem(t, 2)

    def along_y(step):
        return (lax.rem(t + step + NY, NY), e)

    def along_z(step):
        return (t, (x * NZ + lax.rem(z + step + NZ, NZ)) * NC + c)

    def in_row(j):
        return (t, ((j // NC) * NZ + z) * NC + lax.rem(j, NC))

    def other(i):
        return lax.rem(me + i, ROW)

    def send(src, dst, ss, rs, dev):
        return pltpu.make_async_remote_copy(
            src_ref=src, dst_ref=dst, send_sem=ss, recv_sem=rs, device_id=dev, device_id_type=MESH
        )

    def got(ref, sem):
        send(ref, ref, sem, sem, along_y(1)).wait_recv()

    def sent(ref, sem):
        send(ref, ref, sem, sem, along_y(1)).wait_send()

    def offset(d):
        return ((d + 1) // 2) * (1 - 2 * lax.rem(d + 1, 2))

    barrier = pltpu.get_barrier_semaphore()
    for step in (1, 7, 2, 6, 4):
        pl.semaphore_signal(barrier, inc=1, device_id=along_y(step), device_id_type=MESH)
    for i in range(1, ROW):
        pl.semaphore_signal(barrier, inc=1, device_id=in_row(other(i)), device_id_type=MESH)
    for step in range(1, NZ):
        pl.semaphore_signal(barrier, inc=1, device_id=along_z(step), device_id_type=MESH)
    def column(j, parity):
        return pl.ds(pl.multiple_of((2 * j + parity) * SLICE, SLICE), SLICE)

    local = []
    for a, ref in enumerate((gate, up)):
        for j in range(4):
            local.append(
                pltpu.make_async_copy(
                    ref.at[:, column(j, q)],
                    weights.at[pl.ds(a * HID, HID), pl.ds(j * SLICE, SLICE)],
                    lw.at[a, j],
                )
            )
    local.append(pltpu.make_async_copy(down, down_v, ld.at[0]))
    for cp in local:
        cp.start()
    pl.semaphore_wait(barrier, 5 + 7 + 7)

    my_cols = pl.ds(pl.multiple_of((t // 2) * SLICE, SLICE), SLICE)
    for i in range(1, 4):
        send(tok, blocks.at[0, :, my_cols], pg_s.at[i - 1], pg_r.at[i - 1], along_y(2 * i)).start()
    blocks[0, :, my_cols] = tok[...]

    lane = lax.broadcasted_iota(jnp.int32, (ROWS, META), 1).astype(F32)
    idf = ids[...].astype(F32)
    pf = prob[...]
    named = jnp.zeros((ROWS, META), F32)
    for k in range(8):
        named = named + (lane == idf[:, k : k + 1]).astype(F32)
    earlier = (
        lax.broadcasted_iota(jnp.int32, (ROWS, ROWS), 1)
        < lax.broadcasted_iota(jnp.int32, (ROWS, ROWS), 0)
    ).astype(F32)
    before = dot(earlier.astype(BF16), named.astype(BF16), 1, 0)
    meta = jnp.zeros((ROWS, META), F32)
    p_hi = pf.astype(BF16).astype(F32)
    p_lo = pf - p_hi
    for k in range(8):
        ek = idf[:, k : k + 1]
        slot = jnp.sum(jnp.where(lane == ek, before, 0.0), axis=1, keepdims=True)
        meta = jnp.where(lane == float(k), ek, meta)
        meta = jnp.where(lane == float(8 + k), slot, meta)
        meta = jnp.where(lane == float(16 + k), p_hi[:, k : k + 1], meta)
        meta = jnp.where(lane == float(24 + k), p_lo[:, k : k + 1], meta)
    blocks[0, :, pl.ds(HALF, META)] = meta.astype(BF16)
    for i in range(1, 4):
        src = lax.rem(t - 2 * i + NY, NY)
        cols = pl.ds(pl.multiple_of((src // 2) * SLICE, SLICE), SLICE)
        got(blocks.at[0, :, cols], pg_r.at[i - 1])

    lane_i = lax.broadcasted_iota(jnp.int32, (ROWS, META), 1)
    lane_j = lane_i // SLOTS
    lane_e = ((lane_j // NC) * NZ + z) * NC + lax.rem(lane_j, NC)
    lane_code = (lane_e * SLOTS + lax.rem(lane_i, SLOTS)).astype(F32)

    def matches(m):
        return [
            (m[:, k : k + 1] * float(SLOTS) + m[:, 8 + k : 9 + k]) == lane_code for k in range(8)
        ]

    def pass_on(d, whole_to, direction):
        send(
            blocks.at[d], blocks.at[whole_to], z_s.at[whole_to], z_r.at[whole_to], along_z(direction)
        ).start()

    def block_step(d, _):
        @pl.when(jnp.logical_and(d >= 1, d <= 6))
        def _():
            got(blocks.at[d], z_r.at[d])

        @pl.when(d == 7)
        def _():
            got(blocks.at[7, pl.ds(0, 32)], z_r.at[7])
            got(blocks.at[7, pl.ds(32, 32)], z_r.at[8])

        @pl.when(d == 0)
        def _():
            pass_on(0, 1, -1)
            pass_on(0, 2, 1)

        @pl.when(jnp.logical_and(d >= 1, d <= 4))
        def _():
            pass_on(d, d + 2, 1 - 2 * lax.rem(d, 2))

        @pl.when(d == 5)
        def _():
            half = pl.ds(0, 32)
            send(blocks.at[5, half], blocks.at[7, half], z_s.at[7], z_r.at[7], along_z(-1)).start()

        @pl.when(d == 6)
        def _():
            half = pl.ds(32, 32)
            send(blocks.at[6, half], blocks.at[7, half], z_s.at[8], z_r.at[8], along_z(1)).start()

        m = blocks[d, :, pl.ds(HALF, META)].astype(F32)
        pick = functools.reduce(jnp.logical_or, matches(m))
        pick = jnp.where(pick, 1.0, 0.0).astype(BF16)
        rows = dot(pick, blocks[d, :, pl.ds(0, HALF)], 0, 0).astype(BF16)
        picked[d] = rows.reshape(ROW, SLOTS, HALF)
        g = d // 2
        at = pl.ds(pl.multiple_of(lax.rem(d, 2) * SLOTS, SLOTS), SLOTS)
        arrived[g, me, at] = picked[d, me]
        for i in range(1, ROW):
            j = other(i)
            send(
                picked.at[d, j], arrived.at[g, me, at], x_s.at[d, j], x_r.at[d, me], in_row(j)
            ).start()
        return 0

    block_step(0, 0)

    for a, ref in enumerate((gate, up)):
        for j in range(4):
            cols = column(j, 1 - q)
            to = pl.ds(j * SLICE, SLICE)
            send(
                ref.at[pl.ds(0, PIECE), cols],
                weights.at[pl.ds(3 * HID + a * PIECE, PIECE), to],
                w_s.at[0, a, j], w_r.at[0, a, j], along_y(-1),
            ).start()
            send(
                ref.at[pl.ds(PIECE, PIECE), cols],
                weights.at[pl.ds(2 * HID + a * PIECE, PIECE), to],
                w_s.at[1, a, j], w_r.at[1, a, j], along_y(1),
            ).start()

    lax.fori_loop(1, 5, block_step, 0)

    for cp in local:
        cp.wait()
    for a in range(2):
        for j in range(4):
            to = pl.ds(j * SLICE, SLICE)
            got(weights.at[pl.ds(3 * HID + a * PIECE, PIECE), to], w_r.at[0, a, j])
            got(weights.at[pl.ds(2 * HID + a * PIECE, PIECE), to], w_r.at[1, a, j])

    def partials(g):
        for dl in range(2):
            for i in range(1, ROW):
                src = other(i)
                got(arrived.at[g, src, pl.ds(dl * SLOTS, SLOTS)], x_r.at[2 * g + dl, src])
        rows = arrived[g].reshape(2 * ROW * SLOTS, HALF)
        for side in range(2):
            w = weights[pl.ds((2 + side) * HID, HID)]
            part_out[g, side] = dot(w, rows, 1, 1).astype(BF16)
            send(
                part_out.at[g, side], part_in.at[g, 1 - side],
                p_s.at[g, side], p_r.at[g, 1 - side], along_y(2 * side - 1),
            ).start()
        for a in range(2):
            own[pl.ds(a * HID, HID)] = dot(weights[pl.ds(a * HID, HID)], rows, 1, 1)

    def activate(g):
        for side in range(2):
            got(part_in.at[g, side], p_r.at[g, side])
            lo = pl.ds(side * PIECE, PIECE)
            gv = own[lo] + part_in[g, side, pl.ds(0, PIECE)].astype(F32)
            uv = own[pl.ds(HID + side * PIECE, PIECE)] + part_in[
                g, side, pl.ds(PIECE, PIECE)
            ].astype(F32)
            hidden[g, t, lo] = (gv / (1.0 + jnp.exp(-gv)) * uv).astype(BF16)
        for way in range(2):
            send(
                hidden.at[g, t], hidden.at[g, t], h_s.at[g, way, 0], h_r.at[g, way, 0],
                along_y(1 - 2 * way),
            ).start()

    def forward(g, h):
        for way in range(2):
            src = lax.rem(t + (h if way else NY - h), NY)
            ref = hidden.at[g, src]
            got(ref, h_r.at[g, way, h - 1])
            if h == 3:
                ref = hidden.at[g, src, pl.ds(way * PIECE, PIECE)]
            send(ref, ref, h_s.at[g, way, h], h_r.at[g, way, h], along_y(1 - 2 * way)).start()

    def project(g):
        far = lax.rem(t + 4, NY)
        for way in range(2):
            got(hidden.at[g, far, pl.ds(way * PIECE, PIECE)], h_r.at[g, way, 3])
        h = hidden[g].reshape(NY * HID, 2 * ROW * SLOTS)
        o = dot(h, down_v[...], 0, 0).astype(BF16)
        outputs[g] = o.reshape(ROW, 2 * SLOTS, SLICE)
        returned[g, me] = outputs[g, me]
        for i in range(1, ROW):
            j = other(i)
            send(
                outputs.at[g, j], returned.at[g, me], o_s.at[g, j], o_r.at[g, me], in_row(j)
            ).start()

    def combine(g):
        for i in range(1, ROW):
            src = other(i)
            got(returned.at[g, src], o_r.at[g, src])
        for dl in range(2):
            d = 2 * g + dl
            m = blocks[d, :, pl.ds(HALF, META)].astype(F32)
            hi = jnp.zeros((ROWS, META), F32)
            lo = jnp.zeros((ROWS, META), F32)
            for k, match in enumerate(matches(m)):
                hi = jnp.where(match, m[:, 16 + k : 17 + k], hi)
                lo = jnp.where(match, m[:, 24 + k : 25 + k], lo)
            vals = returned[g, :, pl.ds(dl * SLOTS, SLOTS)].reshape(ROW * SLOTS, SLICE)
            total = dot(hi.astype(BF16), vals, 1, 0) + dot(lo.astype(BF16), vals, 1, 0)
            sums_out[d] = total.astype(BF16)

            @pl.when(d == 0)
            def _():
                own_sum[...] = total

            @pl.when(d > 0)
            def _():
                send(
                    sums_out.at[d], sums_in.at[d], f_s.at[d], f_r.at[d], along_z(offset(d))
                ).start()

    def group_step(g, _):
        late = jnp.logical_and(g >= 1, g <= GROUPS)

        @pl.when(g < GROUPS)
        def _():
            partials(g)

        @pl.when(g == 0)
        def _():
            lax.fori_loop(5, 7, block_step, 0)

        @pl.when(g == 1)
        def _():
            block_step(7, 0)

        @pl.when(late)
        def _():
            forward(g - 1, 2)

        @pl.when(g < GROUPS)
        def _():
            activate(g)

        @pl.when(g >= 2)
        def _():
            combine(g - 2)

        @pl.when(late)
        def _():
            forward(g - 1, 3)

        @pl.when(g < GROUPS)
        def _():
            forward(g, 1)

        @pl.when(late)
        def _():
            project(g - 1)

        return 0

    lax.fori_loop(0, GROUPS + 2, group_step, 0)

    total = own_sum[...]
    for d in range(1, NZ):
        got(sums_in.at[d], f_r.at[d])
        total = total + sums_in[d].astype(F32)
    out[...] = total.astype(BF16)

    for i in range(3):
        sent(tok, pg_s.at[i])
    for a in range(2):
        for j in range(4):
            for way in range(2):
                sent(weights.at[pl.ds(0, PIECE), pl.ds(0, SLICE)], w_s.at[way, a, j])
    for d in range(1, 7):
        sent(blocks.at[d], z_s.at[d])
    for d in (7, 8):
        sent(blocks.at[7, pl.ds(0, 32)], z_s.at[d])

    def drain_x(d, _):
        for i in range(1, ROW):
            j = other(i)
            sent(picked.at[d, j], x_s.at[d, j])
        return 0

    lax.fori_loop(0, NZ, drain_x, 0)

    def drain_group(g, _):
        for side in range(2):
            sent(part_out.at[g, side], p_s.at[g, side])
            for h in range(3):
                sent(hidden.at[g, 0], h_s.at[g, side, h])
            sent(hidden.at[g, 0, pl.ds(0, PIECE)], h_s.at[g, side, 3])
        for i in range(1, ROW):
            j = other(i)
            sent(outputs.at[g, j], o_s.at[g, j])
        return 0

    lax.fori_loop(0, GROUPS, drain_group, 0)
    for d in range(1, NZ):
        sent(sums_out.at[d], f_s.at[d])


def local(tokens, gate_weight, up_weight, down_weight, expert_ids, gate_probs):
    hbm = pl.BlockSpec(memory_space=pl.ANY)
    vmem = pl.BlockSpec(memory_space=pltpu.VMEM)
    dma = pltpu.SemaphoreType.DMA
    group_rows = 2 * ROW * SLOTS
    scratch = [
        pltpu.VMEM((NZ, ROWS, HALF + META), BF16),
        pltpu.VMEM((NZ, ROW, SLOTS, HALF), BF16),
        pltpu.VMEM((GROUPS, ROW, 2 * SLOTS, HALF), BF16),
        pltpu.VMEM((4 * HID, HALF), BF16),
        pltpu.VMEM((NY * HID, SLICE), BF16),
        pltpu.VMEM((2 * HID, group_rows), F32),
        pltpu.VMEM((GROUPS, 2, HID, group_rows), BF16),
        pltpu.VMEM((GROUPS, 2, HID, group_rows), BF16),
        pltpu.VMEM((GROUPS, NY, HID, group_rows), BF16),
        pltpu.VMEM((GROUPS, ROW, 2 * SLOTS, SLICE), BF16),
        pltpu.VMEM((GROUPS, ROW, 2 * SLOTS, SLICE), BF16),
        pltpu.VMEM((NZ, ROWS, SLICE), BF16),
        pltpu.VMEM((NZ, ROWS, SLICE), BF16),
        pltpu.VMEM((ROWS, SLICE), F32),
        dma((3,)), dma((3,)),
        dma((2, 2, 4)), dma((2, 2, 4)), dma((2, 4)), dma((1,)),
        dma((9,)), dma((9,)),
        dma((NZ, ROW)), dma((NZ, ROW)),
        dma((GROUPS, 2)), dma((GROUPS, 2)),
        dma((GROUPS, 2, 4)), dma((GROUPS, 2, 4)),
        dma((GROUPS, ROW)), dma((GROUPS, ROW)),
        dma((NZ,)), dma((NZ,)),
    ]
    return pl.pallas_call(
        kernel,
        out_shape=jax.ShapeDtypeStruct((ROWS, SLICE), BF16),
        in_specs=[vmem, hbm, hbm, hbm, vmem, vmem],
        out_specs=vmem,
        scratch_shapes=scratch,
        compiler_params=pltpu.CompilerParams(
            collective_id=0, has_side_effects=True, vmem_limit_bytes=48 << 20
        ),
        cost_estimate=pl.CostEstimate(flops=5_000_000_000, bytes_accessed=5_000_000, transcendentals=200_000),
    )(tokens, gate_weight[0], up_weight[0], down_weight[0], expert_ids, gate_probs)


def solution(mesh):
    in_specs = (
        P("expert", "tensor"),
        P("expert", "tensor", None),
        P("expert", "tensor", None),
        P("expert", None, "tensor"),
        P("expert", None),
        P("expert", None),
    )
    out_specs = P("expert", "tensor")
    return jax.shard_map(local, mesh=mesh, in_specs=in_specs, out_specs=out_specs, check_vma=False)
```

```python
import functools

import jax
import jax.numpy as jnp
from jax import lax
from jax.experimental import pallas as pl
from jax.experimental.pallas import tpu as pltpu
from jax.sharding import PartitionSpec as P

MESH = pl.DeviceIdType.MESH
BF16 = jnp.bfloat16
F32 = jnp.float32
NX, NY, NZ, NC = 4, 8, 8, 2
ROW = NX * NC
ROWS = 64
SLOTS = 16
SLICE = 512
HALF = 2048
HID = 192
PIECE = HID // 2
META = 128
FIRST = META + SLICE
REST = HALF - SLICE
PLACES = (0, 6, 2, 4)
GROUP_ROWS = ROW * SLOTS

ORDER = (
    "M0", "M1", "M2", "G1", "G2", "V0", "M3", "M4", "G3", "M5", "M6", "Z1",
    "Z2", "M7", "B2", "Z3", "Z4", "B3", "B4", "W0", "A0", "A2", "Z5", "Z6",
    "B5", "S0", "B6", "A3", "S2", "Z7", "B7", "10", "B1", "A4", "S3", "12",
    "20", "A5", "S4", "13", "22", "30", "A6", "S5", "14", "23", "32", "A7",
    "S6", "P0", "15", "24", "33", "A1", "S7", "P2", "16", "C0", "25", "34",
    "P3", "S1", "17", "C2", "26", "35", "P4", "11", "C3", "27", "36", "P5",
    "21", "C4", "37", "P6", "31", "C5", "P7", "C6", "P1", "C7", "D0", "D2",
    "D3", "D4", "D5", "D6", "D7", "C1",
)
DIRECT = ()


def dot(a, b, da, db):
    return lax.dot_general(a, b, (((da,), (db,)), ((), ())), preferred_element_type=F32)


def kernel(
    tok, gate, up, down, ids, prob, out,
    blocks, picked, arrived, weights, down_v, own, part_out, part_in,
    hidden, outputs, returned, sums_out, sums_in, own_sum, ids_v, prob_v,
    lt, pg_s, pg_r, w_s, w_r, lw, ld, zs_s, zs_r, zf_s, zf_r, z_s, z_r, xs_s, xs_r, xf_s, xf_r, x_s, x_r, p_s, p_r, h_s, h_r, o_s, o_r, f_s, f_r,
):
    t = lax.axis_index("tensor")
    e = lax.axis_index("expert")
    c = lax.rem(e, NC)
    z = lax.rem(e // NC, NZ)
    x = e // (NC * NZ)
    me = x * NC + c

    def along_y(step):
        return (lax.rem(t + step + NY, NY), e)

    def along_z(step):
        return (t, (x * NZ + lax.rem(z + step + NZ, NZ)) * NC + c)

    def in_row(j):
        return (t, ((j // NC) * NZ + z) * NC + lax.rem(j, NC))

    def other(i):
        return lax.rem(me + i, ROW)

    def send(src, dst, ss, rs, dev):
        return pltpu.make_async_remote_copy(
            src_ref=src, dst_ref=dst, send_sem=ss, recv_sem=rs, device_id=dev, device_id_type=MESH
        )

    def got(ref, sem):
        send(ref, ref, sem, sem, along_y(1)).wait_recv()

    def sent(ref, sem):
        send(ref, ref, sem, sem, along_y(1)).wait_send()

    def offset(d):
        return ((d + 1) // 2) * (1 - 2 * lax.rem(d + 1, 2))

    barrier = pltpu.get_barrier_semaphore()
    for step in range(1, NY):
        pl.semaphore_signal(barrier, inc=1, device_id=along_y(step), device_id_type=MESH)
    for i in range(1, ROW):
        pl.semaphore_signal(barrier, inc=1, device_id=in_row(other(i)), device_id_type=MESH)
    for step in range(1, NZ):
        pl.semaphore_signal(barrier, inc=1, device_id=along_z(step), device_id_type=MESH)
    def column(tensor, p):
        return pl.ds(pl.multiple_of(lax.rem(tensor + PLACES[p], NY) * SLICE, SLICE), SLICE)

    def place(p):
        return pl.ds(META + p * SLICE, SLICE)

    local = []
    for a, ref in enumerate((gate, up)):
        for p in range(4):
            local.append(
                pltpu.make_async_copy(
                    ref.at[:, column(t, p)],
                    weights.at[pl.ds(a * HID, HID), pl.ds(p * SLICE, SLICE)],
                    lw.at[a, p],
                )
            )
    local.append(pltpu.make_async_copy(down, down_v, ld.at[0]))
    first = [
        pltpu.make_async_copy(ids, ids_v, lt.at[0]),
        pltpu.make_async_copy(prob, prob_v, lt.at[1]),
        pltpu.make_async_copy(tok, blocks.at[0, :, place(0)], lt.at[2]),
    ]
    for cp in first + local:
        cp.start()
    for cp in first:
        cp.wait()

    lane = lax.broadcasted_iota(jnp.int32, (ROWS, META), 1).astype(F32)
    p_t = prob_v[...]
    p_hi = p_t.astype(BF16).astype(F32)
    terms = jnp.concatenate([ids_v[...].astype(F32), jnp.zeros((8, ROWS), F32), p_hi, p_t - p_hi], axis=0)
    put = (
        lax.broadcasted_iota(jnp.int32, (32, META), 0) == lax.broadcasted_iota(jnp.int32, (32, META), 1)
    ).astype(F32)
    meta = dot(terms.astype(BF16), put.astype(BF16), 0, 0)
    idf = meta[:, 0:8]
    named = jnp.zeros((ROWS, META), F32)
    for k in range(8):
        named = named + (lane == idf[:, k : k + 1]).astype(F32)
    earlier = (
        lax.broadcasted_iota(jnp.int32, (ROWS, ROWS), 1)
        < lax.broadcasted_iota(jnp.int32, (ROWS, ROWS), 0)
    ).astype(F32)
    before = dot(earlier.astype(BF16), named.astype(BF16), 1, 0)
    for k in range(8):
        ek = idf[:, k : k + 1]
        slot = jnp.sum(jnp.where(lane == ek, before, 0.0), axis=1, keepdims=True)
        meta = jnp.where(lane == float(8 + k), slot, meta)
    blocks[0, :, pl.ds(0, META)] = meta.astype(BF16)
    lane_i = lax.broadcasted_iota(jnp.int32, (ROWS, META), 1)
    lane_j = lane_i // SLOTS
    lane_e = ((lane_j // NC) * NZ + z) * NC + lax.rem(lane_j, NC)
    lane_code = (lane_e * SLOTS + lax.rem(lane_i, SLOTS)).astype(F32)

    def matches(m):
        return [
            (m[:, k : k + 1] * float(SLOTS) + m[:, 8 + k : 9 + k]) == lane_code for k in range(8)
        ]

    def picks(m):
        pick = functools.reduce(jnp.logical_or, matches(m))
        return jnp.where(pick, 1.0, 0.0).astype(BF16)

    own_pick = picks(meta)

    def pick(d, mask, p, n):
        rows = dot(mask, blocks[d, :, pl.ds(META + p * SLICE, n * SLICE)], 0, 0).astype(BF16)
        cols = pl.ds(p * SLICE, n * SLICE)
        picked[d, :, :, cols] = rows.reshape(ROW, SLOTS, n * SLICE)
        arrived[d, me, :, cols] = picked[d, me, :, cols]

    def send_row(d, p, n, ss, rs):
        cols = pl.ds(p * SLICE, n * SLICE)
        for i in range(1, ROW):
            j = other(i)
            send(
                picked.at[d, j, :, cols], arrived.at[d, me, :, cols], ss.at[j], rs.at[me], in_row(j)
            ).start()

    def pass_on(d, cols, ss, rs):
        way = 1 - 2 * (d % 2)
        if d in (5, 6):
            part = pl.ds(32 * (d - 5), 32)
            send(
                blocks.at[d, part, cols], blocks.at[7, part, cols],
                ss.at[d + 2], rs.at[d + 2], along_z(way),
            ).start()
        elif d < 5:
            send(
                blocks.at[d, :, cols], blocks.at[d + 2, :, cols],
                ss.at[d + 2], rs.at[d + 2], along_z(way),
            ).start()

    def block_there(d, cols, rs):
        if d == 7:
            for part in range(2):
                got(blocks.at[7, pl.ds(32 * part, 32), cols], rs.at[7 + part])
        else:
            got(blocks.at[d, :, cols], rs.at[d])

    first_cols = pl.ds(0, FIRST)
    rest_cols = pl.ds(FIRST, REST)

    def mask_of(d):
        return own_pick if d == 0 else picks(blocks[d, :, pl.ds(0, META)].astype(F32))

    def first_step(d):
        if d == 0:
            for way in range(2):
                send(
                    blocks.at[0, :, first_cols], blocks.at[1 + way, :, first_cols],
                    zf_s.at[1 + way], zf_r.at[1 + way], along_z(2 * way - 1),
                ).start()
        else:
            block_there(d, first_cols, zf_r)
            pass_on(d, first_cols, zf_s, zf_r)
            pick(d, mask_of(d), 0, 1)
        send_row(d, 0, 1, xf_s.at[d], xf_r.at[d])

    def gather_step(p):
        got(blocks.at[0, :, place(p)], pg_r.at[p - 1])
        for way in range(2):
            send(
                blocks.at[0, :, place(p)], blocks.at[1 + way, :, place(p)],
                zs_s.at[way, p - 1], zs_r.at[way, p - 1], along_z(2 * way - 1),
            ).start()
        pick(0, own_pick, p, 1)
        send_row(0, p, 1, xs_s.at[p - 1], xs_r.at[p - 1])

    def rest_step(d):
        if d <= 2:
            for p in range(1, 4):
                got(blocks.at[d, :, place(p)], zs_r.at[d - 1, p - 1])
        else:
            block_there(d, rest_cols, z_r)
        pass_on(d, rest_cols, z_s, z_r)

    def block_step(d):
        pick(d, mask_of(d), 1, 3)
        send_row(d, 1, 3, x_s.at[d], x_r.at[d])

    pick(0, own_pick, 0, 1)
    pl.semaphore_wait(barrier, NY + ROW + NZ - 3)

    for p in (3, 1, 2):
        send(
            blocks.at[0, :, place(0)], blocks.at[0, :, place(p)],
            pg_s.at[p - 1], pg_r.at[p - 1], along_y(-PLACES[p]),
        ).start()

    def swap_weights():
        for a, ref in enumerate((gate, up)):
            for p in range(4):
                to = pl.ds(p * SLICE, SLICE)
                send(
                    ref.at[pl.ds(0, PIECE), column(t + NY - 1, p)],
                    weights.at[pl.ds(3 * HID + a * PIECE, PIECE), to],
                    w_s.at[0, a, p], w_r.at[0, a, p], along_y(-1),
                ).start()
                send(
                    ref.at[pl.ds(PIECE, PIECE), column(t + 1, p)],
                    weights.at[pl.ds(2 * HID + a * PIECE, PIECE), to],
                    w_s.at[1, a, p], w_r.at[1, a, p], along_y(1),
                ).start()

    def weights_there():
        for cp in local:
            cp.wait()
        for a in range(2):
            for j in range(4):
                to = pl.ds(j * SLICE, SLICE)
                got(weights.at[pl.ds(3 * HID + a * PIECE, PIECE), to], w_r.at[0, a, j])
                got(weights.at[pl.ds(2 * HID + a * PIECE, PIECE), to], w_r.at[1, a, j])

    def partials(g):
        for i in range(1, ROW):
            src = other(i)
            got(arrived.at[g, src, :, pl.ds(0, SLICE)], xf_r.at[g, src])
            if g == 0:
                for p in range(1, 4):
                    got(arrived.at[0, src, :, pl.ds(p * SLICE, SLICE)], xs_r.at[p - 1, src])
            else:
                got(arrived.at[g, src, :, pl.ds(SLICE, REST)], x_r.at[g, src])
        rows = arrived[g].reshape(GROUP_ROWS, HALF)
        part = dot(weights[pl.ds(2 * HID, 2 * HID)], rows, 1, 1).astype(BF16)
        for side in range(2):
            part_out[g, side] = part[side * HID : (side + 1) * HID]
            send(
                part_out.at[g, side], part_in.at[g, 1 - side],
                p_s.at[g, side], p_r.at[g, 1 - side], along_y(2 * side - 1),
            ).start()
        own[g] = dot(weights[pl.ds(0, 2 * HID)], rows, 1, 1)

    def activate(g):
        for side in range(2):
            got(part_in.at[g, side], p_r.at[g, side])
            lo = pl.ds(side * PIECE, PIECE)
            gv = own[g, lo] + part_in[g, side, pl.ds(0, PIECE)].astype(F32)
            uv = own[g, pl.ds(HID + side * PIECE, PIECE)] + part_in[
                g, side, pl.ds(PIECE, PIECE)
            ].astype(F32)
            hidden[g, t, lo] = (gv / (1.0 + jnp.exp(-gv)) * uv).astype(BF16)
        if g in DIRECT:
            for step in (4, 1, 7, 2, 6, 3, 5):
                sem = (step // 5, 3 - abs(4 - step) if step < 5 else 7 - step)
                send(
                    hidden.at[g, t], hidden.at[g, t], h_s.at[g, sem[0], sem[1]],
                    h_r.at[g, sem[0], sem[1]], along_y(step),
                ).start()
            return
        for way in range(2):
            send(
                hidden.at[g, t], hidden.at[g, t], h_s.at[g, way, 0], h_r.at[g, way, 0],
                along_y(1 - 2 * way),
            ).start()

    def forward(g, h):
        for way in range(2):
            src = lax.rem(t + (h if way else NY - h), NY)
            ref = hidden.at[g, src]
            got(ref, h_r.at[g, way, h - 1])
            if h == 3:
                ref = hidden.at[g, src, pl.ds(way * PIECE, PIECE)]
            send(ref, ref, h_s.at[g, way, h], h_r.at[g, way, h], along_y(1 - 2 * way)).start()

    def project(g):
        if g in DIRECT:
            for step in range(1, NY):
                sem = (step // 5, 3 - abs(4 - step) if step < 5 else 7 - step)
                got(hidden.at[g, lax.rem(t + NY - step, NY)], h_r.at[g, sem[0], sem[1]])
        else:
            far = lax.rem(t + 4, NY)
            for way in range(2):
                got(hidden.at[g, far, pl.ds(way * PIECE, PIECE)], h_r.at[g, way, 3])
        h = hidden[g].reshape(NY * HID, GROUP_ROWS)
        o = dot(h, down_v[...], 0, 0).astype(BF16)
        outputs[g] = o.reshape(ROW, SLOTS, SLICE)
        returned[g, me] = outputs[g, me]
        for i in range(1, ROW):
            j = other(i)
            send(
                outputs.at[g, j], returned.at[g, me], o_s.at[g, j], o_r.at[g, me], in_row(j)
            ).start()

    def combine(g):
        for i in range(1, ROW):
            src = other(i)
            got(returned.at[g, src], o_r.at[g, src])
        m = blocks[g, :, pl.ds(0, META)].astype(F32)
        hi = jnp.zeros((ROWS, META), F32)
        lo = jnp.zeros((ROWS, META), F32)
        for k, match in enumerate(matches(m)):
            hi = jnp.where(match, m[:, 16 + k : 17 + k], hi)
            lo = jnp.where(match, m[:, 24 + k : 25 + k], lo)
        vals = returned[g].reshape(GROUP_ROWS, SLICE)
        total = dot(hi.astype(BF16), vals, 1, 0) + dot(lo.astype(BF16), vals, 1, 0)
        sums_out[g] = total.astype(BF16)

        if g == 0:
            own_sum[...] = total
        else:
            send(sums_out.at[g], sums_in.at[g], f_s.at[g], f_r.at[g], along_z(offset(g))).start()

    def drain(g):
        for i in range(1, ROW):
            j = other(i)
            sent(picked.at[g, j, :, pl.ds(0, SLICE)], xf_s.at[g, j])
            if g == 0:
                for p in range(1, 4):
                    sent(picked.at[0, j, :, pl.ds(p * SLICE, SLICE)], xs_s.at[p - 1, j])
            else:
                sent(picked.at[g, j, :, pl.ds(SLICE, REST)], x_s.at[g, j])
        for side in range(2):
            sent(part_out.at[g, side], p_s.at[g, side])
            for h in range(3):
                sent(hidden.at[g, 0], h_s.at[g, side, h])
        if g in DIRECT:
            sent(hidden.at[g, 0], h_s.at[g, 0, 3])
        else:
            for side in range(2):
                sent(hidden.at[g, 0, pl.ds(0, PIECE)], h_s.at[g, side, 3])
        for i in range(1, ROW):
            j = other(i)
            sent(outputs.at[g, j], o_s.at[g, j])

    run = {
        "M": first_step, "G": gather_step, "Z": rest_step, "B": block_step, "V": lambda k: swap_weights(), "A": partials, "S": activate, "P": project, "C": combine, "D": drain,
        "1": lambda k: forward(k, 1), "2": lambda k: forward(k, 2), "3": lambda k: forward(k, 3),
        "W": lambda k: weights_there(),
    }
    for step in ORDER:
        run[step[0]](int(step[1]))

    drain(1)
    for i in range(3):
        sent(blocks.at[0, :, place(0)], pg_s.at[i])
    for a in range(2):
        for j in range(4):
            for way in range(2):
                sent(weights.at[pl.ds(0, PIECE), pl.ds(0, SLICE)], w_s.at[way, a, j])
    for way in range(2):
        for p in range(1, 4):
            sent(blocks.at[0, :, place(p)], zs_s.at[way, p - 1])
        sent(blocks.at[0, :, first_cols], zf_s.at[1 + way])
    for d in range(3, 7):
        sent(blocks.at[d, :, first_cols], zf_s.at[d])
        sent(blocks.at[d, :, rest_cols], z_s.at[d])
    for d in (7, 8):
        sent(blocks.at[7, pl.ds(0, 32), first_cols], zf_s.at[d])
        sent(blocks.at[7, pl.ds(0, 32), rest_cols], z_s.at[d])

    total = own_sum[...]
    for d in (2, 3, 4, 5, 6, 7, 1):
        got(sums_in.at[d], f_r.at[d])
        total = total + sums_in[d].astype(F32)
    out[...] = total.astype(BF16)
    for d in range(1, NZ):
        sent(sums_out.at[d], f_s.at[d])


def local(tokens, gate_weight, up_weight, down_weight, expert_ids, gate_probs):
    hbm = pl.BlockSpec(memory_space=pltpu.HBM)
    vmem = pl.BlockSpec(memory_space=pltpu.VMEM)
    dma = pltpu.SemaphoreType.DMA
    scratch = [
        pltpu.VMEM((NZ, ROWS, HALF + META), BF16),
        pltpu.VMEM((NZ, ROW, SLOTS, HALF), BF16),
        pltpu.VMEM((NZ, ROW, SLOTS, HALF), BF16),
        pltpu.VMEM((4 * HID, HALF), BF16),
        pltpu.VMEM((NY * HID, SLICE), BF16),
        pltpu.VMEM((NZ, 2 * HID, GROUP_ROWS), F32),
        pltpu.VMEM((NZ, 2, HID, GROUP_ROWS), BF16),
        pltpu.VMEM((NZ, 2, HID, GROUP_ROWS), BF16),
        pltpu.VMEM((NZ, NY, HID, GROUP_ROWS), BF16),
        pltpu.VMEM((NZ, ROW, SLOTS, SLICE), BF16),
        pltpu.VMEM((NZ, ROW, SLOTS, SLICE), BF16),
        pltpu.VMEM((NZ, ROWS, SLICE), BF16),
        pltpu.VMEM((NZ, ROWS, SLICE), BF16),
        pltpu.VMEM((ROWS, SLICE), F32),
        pltpu.VMEM((8, ROWS), jnp.int32),
        pltpu.VMEM((8, ROWS), F32),
        dma((3,)),
        dma((3,)), dma((3,)),
        dma((2, 2, 4)), dma((2, 2, 4)), dma((2, 4)), dma((1,)),
        dma((2, 3)), dma((2, 3)), dma((9,)), dma((9,)), dma((9,)), dma((9,)),
        dma((3, ROW)), dma((3, ROW)), dma((NZ, ROW)), dma((NZ, ROW)), dma((NZ, ROW)), dma((NZ, ROW)),
        dma((NZ, 2)), dma((NZ, 2)),
        dma((NZ, 2, 4)), dma((NZ, 2, 4)),
        dma((NZ, ROW)), dma((NZ, ROW)),
        dma((NZ,)), dma((NZ,)),
    ]
    return pl.pallas_call(
        kernel,
        out_shape=jax.ShapeDtypeStruct((ROWS, SLICE), BF16),
        in_specs=[hbm] * 6,
        out_specs=vmem,
        scratch_shapes=scratch,
        compiler_params=pltpu.CompilerParams(
            collective_id=0, has_side_effects=True, vmem_limit_bytes=(64 << 20) - (1 << 18)
        ),
        cost_estimate=pl.CostEstimate(flops=5_000_000_000, bytes_accessed=5_000_000, transcendentals=200_000),
    )(tokens, gate_weight[0], up_weight[0], down_weight[0], expert_ids.T, gate_probs.T)


def solution(mesh):
    in_specs = (
        P("expert", "tensor"),
        P("expert", "tensor", None),
        P("expert", "tensor", None),
        P("expert", None, "tensor"),
        P("expert", None),
        P("expert", None),
    )
    out_specs = P("expert", "tensor")
    return jax.shard_map(local, mesh=mesh, in_specs=in_specs, out_specs=out_specs, check_vma=False)
```

```python
import functools

import jax
import jax.numpy as jnp
from jax import lax
from jax.experimental import pallas as pl
from jax.experimental.pallas import tpu as pltpu
from jax.sharding import PartitionSpec as P

MESH = pl.DeviceIdType.MESH
BF16 = jnp.bfloat16
F32 = jnp.float32
NX, NY, NZ, NC = 4, 8, 8, 2
ROW = NX * NC
ROWS = 64
SLOTS = 16
SLICE = 512
HALF = 2048
HID = 192
PIECE = HID // 2
META = 128
FIRST = META + SLICE
REST = HALF - SLICE
PLACES = (0, 6, 2, 4)
GROUP_ROWS = ROW * SLOTS

ORDER = (
    "M0", "V0", "M1", "M2", "G1", "G2", "M3", "M4", "G3", "M5", "M6", "Z1",
    "Z2", "M7", "B2", "Z3", "Z4", "B3", "B4", "W0", "A0", "A2", "Z5", "Z6",
    "B5", "S0", "B6", "A3", "S2", "Z7", "B7", "10", "B1", "A4", "S3", "12",
    "20", "A5", "S4", "13", "22", "30", "A6", "S5", "14", "23", "32", "A7",
    "S6", "P0", "15", "24", "33", "A1", "S7", "P2", "16", "C0", "25", "34",
    "P3", "S1", "17", "C2", "26", "35", "P4", "11", "C3", "27", "36", "P5",
    "21", "C4", "37", "P6", "31", "C5", "P7", "C6", "P1", "C7", "D0", "D2",
    "D3", "D4", "D5", "D6", "D7", "C1",
)


def dot(a, b, da, db):
    return lax.dot_general(a, b, (((da,), (db,)), ((), ())), preferred_element_type=F32)


def kernel(
    tok, gate, up, down, ids, prob, out,
    blocks, picked, arrived, weights, down_v, own, part_out, part_in,
    hidden, outputs, returned, sums_out, sums_in, own_sum, ids_v, prob_v,
    lt, pg_s, pg_r, w_s, w_r, lw, ld, zs_s, zs_r, zf_s, zf_r, z_s, z_r, xs_s, xs_r, xf_s, xf_r, x_s, x_r, p_s, p_r, h_s, h_r, o_s, o_r, f_s, f_r,
):
    t = lax.axis_index("tensor")
    e = lax.axis_index("expert")
    c = lax.rem(e, NC)
    z = lax.rem(e // NC, NZ)
    x = e // (NC * NZ)
    me = x * NC + c

    def along_y(step):
        return (lax.rem(t + step + NY, NY), e)

    def along_z(step):
        return (t, (x * NZ + lax.rem(z + step + NZ, NZ)) * NC + c)

    def in_row(j):
        return (t, ((j // NC) * NZ + z) * NC + lax.rem(j, NC))

    def other(i):
        return lax.rem(me + i, ROW)

    def send(src, dst, ss, rs, dev):
        return pltpu.make_async_remote_copy(
            src_ref=src, dst_ref=dst, send_sem=ss, recv_sem=rs, device_id=dev, device_id_type=MESH
        )

    def got(ref, sem):
        send(ref, ref, sem, sem, along_y(1)).wait_recv()

    def sent(ref, sem):
        send(ref, ref, sem, sem, along_y(1)).wait_send()

    def offset(d):
        return ((d + 1) // 2) * (1 - 2 * lax.rem(d + 1, 2))

    barrier = pltpu.get_barrier_semaphore()
    for step in (4, 2, 6, 1, 7):
        pl.semaphore_signal(barrier, inc=1, device_id=along_y(step), device_id_type=MESH)
    for i in (4, 5, 3, 2, 6, 7, 1):
        pl.semaphore_signal(barrier, inc=1, device_id=in_row(other(i)), device_id_type=MESH)
    for step in (4, 3, 5, 2, 6, 1, 7):
        pl.semaphore_signal(barrier, inc=1, device_id=along_z(step), device_id_type=MESH)
    def column(tensor, p):
        return pl.ds(pl.multiple_of(lax.rem(tensor + PLACES[p], NY) * SLICE, SLICE), SLICE)

    def place(p):
        return pl.ds(META + p * SLICE, SLICE)

    local = []
    for a, ref in enumerate((gate, up)):
        for p in range(4):
            local.append(
                pltpu.make_async_copy(
                    ref.at[:, column(t, p)],
                    weights.at[pl.ds(a * HID, HID), pl.ds(p * SLICE, SLICE)],
                    lw.at[a, p],
                )
            )
    local.append(pltpu.make_async_copy(down, down_v, ld.at[0]))
    first = [
        pltpu.make_async_copy(ids, ids_v, lt.at[0]),
        pltpu.make_async_copy(prob, prob_v, lt.at[1]),
        pltpu.make_async_copy(tok, blocks.at[0, :, place(0)], lt.at[2]),
    ]
    for cp in first + local:
        cp.start()
    for cp in first:
        cp.wait()

    lane = lax.broadcasted_iota(jnp.int32, (ROWS, META), 1).astype(F32)
    p_t = prob_v[...]
    p_hi = p_t.astype(BF16).astype(F32)
    terms = jnp.concatenate([ids_v[...].astype(F32), jnp.zeros((8, ROWS), F32), p_hi, p_t - p_hi], axis=0)
    put = (
        lax.broadcasted_iota(jnp.int32, (32, META), 0) == lax.broadcasted_iota(jnp.int32, (32, META), 1)
    ).astype(F32)
    meta = dot(terms.astype(BF16), put.astype(BF16), 0, 0)
    idf = meta[:, 0:8]
    named = jnp.zeros((ROWS, META), F32)
    for k in range(8):
        named = named + (lane == idf[:, k : k + 1]).astype(F32)
    earlier = (
        lax.broadcasted_iota(jnp.int32, (ROWS, ROWS), 1)
        < lax.broadcasted_iota(jnp.int32, (ROWS, ROWS), 0)
    ).astype(F32)
    before = dot(earlier.astype(BF16), named.astype(BF16), 1, 0)
    for k in range(8):
        ek = idf[:, k : k + 1]
        slot = jnp.sum(jnp.where(lane == ek, before, 0.0), axis=1, keepdims=True)
        meta = jnp.where(lane == float(8 + k), slot, meta)
    blocks[0, :, pl.ds(0, META)] = meta.astype(BF16)
    lane_i = lax.broadcasted_iota(jnp.int32, (ROWS, META), 1)
    lane_j = lane_i // SLOTS
    lane_e = ((lane_j // NC) * NZ + z) * NC + lax.rem(lane_j, NC)
    lane_code = (lane_e * SLOTS + lax.rem(lane_i, SLOTS)).astype(F32)

    def matches(m):
        return [
            (m[:, k : k + 1] * float(SLOTS) + m[:, 8 + k : 9 + k]) == lane_code for k in range(8)
        ]

    def picks(m):
        pick = functools.reduce(jnp.logical_or, matches(m))
        return jnp.where(pick, 1.0, 0.0).astype(BF16)

    own_pick = picks(meta)

    def pick(d, mask, p, n):
        rows = dot(mask, blocks[d, :, pl.ds(META + p * SLICE, n * SLICE)], 0, 0).astype(BF16)
        cols = pl.ds(p * SLICE, n * SLICE)
        picked[d, :, :, cols] = rows.reshape(ROW, SLOTS, n * SLICE)
        arrived[d, me, :, cols] = picked[d, me, :, cols]

    def send_row(d, p, n, ss, rs):
        cols = pl.ds(p * SLICE, n * SLICE)
        for i in range(1, ROW):
            j = other(i)
            send(
                picked.at[d, j, :, cols], arrived.at[d, me, :, cols], ss.at[j], rs.at[me], in_row(j)
            ).start()

    def pass_on(d, cols, ss, rs):
        way = 1 - 2 * (d % 2)
        if d in (5, 6):
            part = pl.ds(32 * (d - 5), 32)
            send(
                blocks.at[d, part, cols], blocks.at[7, part, cols],
                ss.at[d + 2], rs.at[d + 2], along_z(way),
            ).start()
        elif d < 5:
            send(
                blocks.at[d, :, cols], blocks.at[d + 2, :, cols],
                ss.at[d + 2], rs.at[d + 2], along_z(way),
            ).start()

    def block_there(d, cols, rs):
        if d == 7:
            for part in range(2):
                got(blocks.at[7, pl.ds(32 * part, 32), cols], rs.at[7 + part])
        else:
            got(blocks.at[d, :, cols], rs.at[d])

    first_cols = pl.ds(0, FIRST)
    rest_cols = pl.ds(FIRST, REST)

    def mask_of(d):
        return own_pick if d == 0 else picks(blocks[d, :, pl.ds(0, META)].astype(F32))

    def first_step(d):
        if d == 0:
            for way in range(2):
                send(
                    blocks.at[0, :, first_cols], blocks.at[1 + way, :, first_cols],
                    zf_s.at[1 + way], zf_r.at[1 + way], along_z(2 * way - 1),
                ).start()
        else:
            block_there(d, first_cols, zf_r)
            pass_on(d, first_cols, zf_s, zf_r)
            pick(d, mask_of(d), 0, 1)
        send_row(d, 0, 1, xf_s.at[d], xf_r.at[d])

    def gather_step(p):
        got(blocks.at[0, :, place(p)], pg_r.at[p - 1])
        for way in range(2):
            send(
                blocks.at[0, :, place(p)], blocks.at[1 + way, :, place(p)],
                zs_s.at[way, p - 1], zs_r.at[way, p - 1], along_z(2 * way - 1),
            ).start()
        pick(0, own_pick, p, 1)
        send_row(0, p, 1, xs_s.at[p - 1], xs_r.at[p - 1])

    def rest_step(d):
        if d <= 2:
            for p in range(1, 4):
                got(blocks.at[d, :, place(p)], zs_r.at[d - 1, p - 1])
        else:
            block_there(d, rest_cols, z_r)
        pass_on(d, rest_cols, z_s, z_r)

    def block_step(d):
        pick(d, mask_of(d), 1, 3)
        send_row(d, 1, 3, x_s.at[d], x_r.at[d])

    pick(0, own_pick, 0, 1)
    pl.semaphore_wait(barrier, 5 + 7 + 7)

    for p in (3, 1, 2):
        send(
            blocks.at[0, :, place(0)], blocks.at[0, :, place(p)],
            pg_s.at[p - 1], pg_r.at[p - 1], along_y(-PLACES[p]),
        ).start()

    def swap_weights():
        for a, ref in enumerate((gate, up)):
            for p in range(4):
                to = pl.ds(p * SLICE, SLICE)
                send(
                    ref.at[pl.ds(0, PIECE), column(t + NY - 1, p)],
                    weights.at[pl.ds(3 * HID + a * PIECE, PIECE), to],
                    w_s.at[0, a, p], w_r.at[0, a, p], along_y(-1),
                ).start()
                send(
                    ref.at[pl.ds(PIECE, PIECE), column(t + 1, p)],
                    weights.at[pl.ds(2 * HID + a * PIECE, PIECE), to],
                    w_s.at[1, a, p], w_r.at[1, a, p], along_y(1),
                ).start()

    def weights_there():
        for cp in local:
            cp.wait()
        for a in range(2):
            for j in range(4):
                to = pl.ds(j * SLICE, SLICE)
                got(weights.at[pl.ds(3 * HID + a * PIECE, PIECE), to], w_r.at[0, a, j])
                got(weights.at[pl.ds(2 * HID + a * PIECE, PIECE), to], w_r.at[1, a, j])

    def partials(g):
        for i in range(1, ROW):
            src = other(i)
            got(arrived.at[g, src, :, pl.ds(0, SLICE)], xf_r.at[g, src])
            if g == 0:
                for p in range(1, 4):
                    got(arrived.at[0, src, :, pl.ds(p * SLICE, SLICE)], xs_r.at[p - 1, src])
            else:
                got(arrived.at[g, src, :, pl.ds(SLICE, REST)], x_r.at[g, src])
        rows = arrived[g].reshape(GROUP_ROWS, HALF)
        part = dot(weights[pl.ds(2 * HID, 2 * HID)], rows, 1, 1).astype(BF16)
        for side in range(2):
            part_out[g, side] = part[side * HID : (side + 1) * HID]
            send(
                part_out.at[g, side], part_in.at[g, 1 - side],
                p_s.at[g, side], p_r.at[g, 1 - side], along_y(2 * side - 1),
            ).start()
        own[g] = dot(weights[pl.ds(0, 2 * HID)], rows, 1, 1)

    def activate(g):
        for side in range(2):
            got(part_in.at[g, side], p_r.at[g, side])
            lo = pl.ds(side * PIECE, PIECE)
            gv = own[g, lo] + part_in[g, side, pl.ds(0, PIECE)].astype(F32)
            uv = own[g, pl.ds(HID + side * PIECE, PIECE)] + part_in[
                g, side, pl.ds(PIECE, PIECE)
            ].astype(F32)
            hidden[g, t, lo] = (gv / (1.0 + jnp.exp(-gv)) * uv).astype(BF16)
        for way in range(2):
            send(
                hidden.at[g, t], hidden.at[g, t], h_s.at[g, way, 0], h_r.at[g, way, 0],
                along_y(1 - 2 * way),
            ).start()

    def forward(g, h):
        for way in range(2):
            src = lax.rem(t + (h if way else NY - h), NY)
            ref = hidden.at[g, src]
            got(ref, h_r.at[g, way, h - 1])
            if h == 3:
                ref = hidden.at[g, src, pl.ds(way * PIECE, PIECE)]
            send(ref, ref, h_s.at[g, way, h], h_r.at[g, way, h], along_y(1 - 2 * way)).start()

    def project(g):
        far = lax.rem(t + 4, NY)
        for way in range(2):
            got(hidden.at[g, far, pl.ds(way * PIECE, PIECE)], h_r.at[g, way, 3])
        h = hidden[g].reshape(NY * HID, GROUP_ROWS)
        o = dot(h, down_v[...], 0, 0).astype(BF16)
        outputs[g] = o.reshape(ROW, SLOTS, SLICE)
        returned[g, me] = outputs[g, me]
        for i in range(1, ROW):
            j = other(i)
            send(
                outputs.at[g, j], returned.at[g, me], o_s.at[g, j], o_r.at[g, me], in_row(j)
            ).start()

    def combine(g):
        for i in range(1, ROW):
            src = other(i)
            got(returned.at[g, src], o_r.at[g, src])
        m = blocks[g, :, pl.ds(0, META)].astype(F32)
        hi = jnp.zeros((ROWS, META), F32)
        lo = jnp.zeros((ROWS, META), F32)
        for k, match in enumerate(matches(m)):
            hi = jnp.where(match, m[:, 16 + k : 17 + k], hi)
            lo = jnp.where(match, m[:, 24 + k : 25 + k], lo)
        vals = returned[g].reshape(GROUP_ROWS, SLICE)
        total = dot(hi.astype(BF16), vals, 1, 0) + dot(lo.astype(BF16), vals, 1, 0)
        sums_out[g] = total.astype(BF16)

        if g == 0:
            own_sum[...] = total
        else:
            send(sums_out.at[g], sums_in.at[g], f_s.at[g], f_r.at[g], along_z(offset(g))).start()

    def drain(g):
        for i in range(1, ROW):
            j = other(i)
            sent(picked.at[g, j, :, pl.ds(0, SLICE)], xf_s.at[g, j])
            if g == 0:
                for p in range(1, 4):
                    sent(picked.at[0, j, :, pl.ds(p * SLICE, SLICE)], xs_s.at[p - 1, j])
            else:
                sent(picked.at[g, j, :, pl.ds(SLICE, REST)], x_s.at[g, j])
        for side in range(2):
            sent(part_out.at[g, side], p_s.at[g, side])
            for h in range(3):
                sent(hidden.at[g, 0], h_s.at[g, side, h])
        for side in range(2):
            sent(hidden.at[g, 0, pl.ds(0, PIECE)], h_s.at[g, side, 3])
        for i in range(1, ROW):
            j = other(i)
            sent(outputs.at[g, j], o_s.at[g, j])

    run = {
        "M": first_step, "G": gather_step, "Z": rest_step, "B": block_step, "V": lambda k: swap_weights(), "A": partials, "S": activate, "P": project, "C": combine, "D": drain,
        "1": lambda k: forward(k, 1), "2": lambda k: forward(k, 2), "3": lambda k: forward(k, 3),
        "W": lambda k: weights_there(),
    }
    for step in ORDER:
        run[step[0]](int(step[1]))

    drain(1)
    for i in range(3):
        sent(blocks.at[0, :, place(0)], pg_s.at[i])
    for a in range(2):
        for j in range(4):
            for way in range(2):
                sent(weights.at[pl.ds(0, PIECE), pl.ds(0, SLICE)], w_s.at[way, a, j])
    for way in range(2):
        for p in range(1, 4):
            sent(blocks.at[0, :, place(p)], zs_s.at[way, p - 1])
        sent(blocks.at[0, :, first_cols], zf_s.at[1 + way])
    for d in range(3, 7):
        sent(blocks.at[d, :, first_cols], zf_s.at[d])
        sent(blocks.at[d, :, rest_cols], z_s.at[d])
    for d in (7, 8):
        sent(blocks.at[7, pl.ds(0, 32), first_cols], zf_s.at[d])
        sent(blocks.at[7, pl.ds(0, 32), rest_cols], z_s.at[d])

    total = own_sum[...]
    for d in (2, 3, 4, 5, 6, 7, 1):
        got(sums_in.at[d], f_r.at[d])
        total = total + sums_in[d].astype(F32)
    out[...] = total.astype(BF16)
    for d in range(1, NZ):
        sent(sums_out.at[d], f_s.at[d])


def local(tokens, gate_weight, up_weight, down_weight, expert_ids, gate_probs):
    hbm = pl.BlockSpec(memory_space=pltpu.HBM)
    vmem = pl.BlockSpec(memory_space=pltpu.VMEM)
    dma = pltpu.SemaphoreType.DMA
    scratch = [
        pltpu.VMEM((NZ, ROWS, HALF + META), BF16),
        pltpu.VMEM((NZ, ROW, SLOTS, HALF), BF16),
        pltpu.VMEM((NZ, ROW, SLOTS, HALF), BF16),
        pltpu.VMEM((4 * HID, HALF), BF16),
        pltpu.VMEM((NY * HID, SLICE), BF16),
        pltpu.VMEM((NZ, 2 * HID, GROUP_ROWS), F32),
        pltpu.VMEM((NZ, 2, HID, GROUP_ROWS), BF16),
        pltpu.VMEM((NZ, 2, HID, GROUP_ROWS), BF16),
        pltpu.VMEM((NZ, NY, HID, GROUP_ROWS), BF16),
        pltpu.VMEM((NZ, ROW, SLOTS, SLICE), BF16),
        pltpu.VMEM((NZ, ROW, SLOTS, SLICE), BF16),
        pltpu.VMEM((NZ, ROWS, SLICE), BF16),
        pltpu.VMEM((NZ, ROWS, SLICE), BF16),
        pltpu.VMEM((ROWS, SLICE), F32),
        pltpu.VMEM((8, ROWS), jnp.int32),
        pltpu.VMEM((8, ROWS), F32),
        dma((3,)),
        dma((3,)), dma((3,)),
        dma((2, 2, 4)), dma((2, 2, 4)), dma((2, 4)), dma((1,)),
        dma((2, 3)), dma((2, 3)), dma((9,)), dma((9,)), dma((9,)), dma((9,)),
        dma((3, ROW)), dma((3, ROW)), dma((NZ, ROW)), dma((NZ, ROW)), dma((NZ, ROW)), dma((NZ, ROW)),
        dma((NZ, 2)), dma((NZ, 2)),
        dma((NZ, 2, 4)), dma((NZ, 2, 4)),
        dma((NZ, ROW)), dma((NZ, ROW)),
        dma((NZ,)), dma((NZ,)),
    ]
    return pl.pallas_call(
        kernel,
        out_shape=jax.ShapeDtypeStruct((ROWS, SLICE), BF16),
        in_specs=[hbm] * 6,
        out_specs=vmem,
        scratch_shapes=scratch,
        compiler_params=pltpu.CompilerParams(
            collective_id=0, has_side_effects=True, vmem_limit_bytes=(64 << 20) - (1 << 18)
        ),
        cost_estimate=pl.CostEstimate(flops=5_000_000_000, bytes_accessed=5_000_000, transcendentals=200_000),
    )(tokens, gate_weight[0], up_weight[0], down_weight[0], expert_ids.T, gate_probs.T)


def solution(mesh):
    in_specs = (
        P("expert", "tensor"),
        P("expert", "tensor", None),
        P("expert", "tensor", None),
        P("expert", None, "tensor"),
        P("expert", None),
        P("expert", None),
    )
    out_specs = P("expert", "tensor")
    return jax.shard_map(local, mesh=mesh, in_specs=in_specs, out_specs=out_specs, check_vma=False)
```

```python
import functools

import jax
import jax.numpy as jnp
from jax import lax
from jax.experimental import pallas as pl
from jax.experimental.pallas import tpu as pltpu
from jax.sharding import PartitionSpec as P

MESH = pl.DeviceIdType.MESH
BF16 = jnp.bfloat16
F32 = jnp.float32
NX, NY, NZ, NC = 4, 8, 8, 2
ROW = NX * NC
ROWS = 64
SLOTS = 16
FAR_FIRST = (4, 5, 3, 2, 6, 7, 1)
SLICE = 512
HALF = 2048
HID = 192
PIECE = HID // 2
META = 128
FIRST = META + SLICE
REST = HALF - SLICE
PLACES = (0, 6, 2, 4)
GROUP_ROWS = ROW * SLOTS

ORDER = (
    "M0", "V0", "M1", "M2", "G1", "G2", "M3", "M4", "G3", "M5", "M6", "Z1",
    "Z2", "M7", "B2", "Z3", "Z4", "B3", "B4", "W0", "A0", "A2", "Z5", "Z6",
    "B5", "S0", "B6", "A3", "S2", "Z7", "B7", "10", "B1", "A4", "S3", "12",
    "20", "A5", "S4", "13", "22", "30", "A6", "S5", "14", "23", "32", "A7",
    "S6", "P0", "15", "24", "33", "A1", "S7", "P2", "16", "C0", "25", "34",
    "P3", "S1", "17", "C2", "26", "35", "P4", "11", "C3", "27", "36", "P5",
    "21", "C4", "37", "P6", "31", "C5", "P7", "C6", "P1", "C7", "D0", "D2",
    "D3", "D4", "D5", "D6", "D7", "C1",
)


def dot(a, b, da, db):
    return lax.dot_general(a, b, (((da,), (db,)), ((), ())), preferred_element_type=F32)


def kernel(
    tok, gate, up, down, ids, prob, out,
    blocks, picked, arrived, weights, down_v, own, part_out, part_in,
    hidden, outputs, returned, sums_out, sums_in, own_sum, ids_v, prob_v,
    lt, pg_s, pg_r, w_s, w_r, lw, ld, zs_s, zs_r, zf_s, zf_r, z_s, z_r, xs_s, xs_r, xf_s, xf_r, x_s, x_r, p_s, p_r, h_s, h_r, o_s, o_r, f_s, f_r,
):
    t = lax.axis_index("tensor")
    e = lax.axis_index("expert")
    c = lax.rem(e, NC)
    z = lax.rem(e // NC, NZ)
    x = e // (NC * NZ)
    me = x * NC + c

    def along_y(step):
        return (lax.rem(t + step + NY, NY), e)

    def along_z(step):
        return (t, (x * NZ + lax.rem(z + step + NZ, NZ)) * NC + c)

    def in_row(j):
        return (t, ((j // NC) * NZ + z) * NC + lax.rem(j, NC))

    def other(i):
        return lax.rem(me + i, ROW)

    def send(src, dst, ss, rs, dev):
        return pltpu.make_async_remote_copy(
            src_ref=src, dst_ref=dst, send_sem=ss, recv_sem=rs, device_id=dev, device_id_type=MESH
        )

    def got(ref, sem):
        send(ref, ref, sem, sem, along_y(1)).wait_recv()

    def sent(ref, sem):
        send(ref, ref, sem, sem, along_y(1)).wait_send()

    def offset(d):
        return ((d + 1) // 2) * (1 - 2 * lax.rem(d + 1, 2))

    barrier = pltpu.get_barrier_semaphore()
    for step in (4, 2, 6, 1, 7):
        pl.semaphore_signal(barrier, inc=1, device_id=along_y(step), device_id_type=MESH)
    for i in FAR_FIRST:
        pl.semaphore_signal(barrier, inc=1, device_id=in_row(other(i)), device_id_type=MESH)
    for step in (4, 3, 5, 2, 6, 1, 7):
        pl.semaphore_signal(barrier, inc=1, device_id=along_z(step), device_id_type=MESH)
    def column(tensor, p):
        return pl.ds(pl.multiple_of(lax.rem(tensor + PLACES[p], NY) * SLICE, SLICE), SLICE)

    def place(p):
        return pl.ds(META + p * SLICE, SLICE)

    local = []
    for a, ref in enumerate((gate, up)):
        for p in range(4):
            local.append(
                pltpu.make_async_copy(
                    ref.at[:, column(t, p)],
                    weights.at[pl.ds(a * HID, HID), pl.ds(p * SLICE, SLICE)],
                    lw.at[a, p],
                )
            )
    local.append(pltpu.make_async_copy(down, down_v, ld.at[0]))
    first = [
        pltpu.make_async_copy(ids, ids_v, lt.at[0]),
        pltpu.make_async_copy(prob, prob_v, lt.at[1]),
        pltpu.make_async_copy(tok, blocks.at[0, :, place(0)], lt.at[2]),
    ]
    for cp in first + local:
        cp.start()
    for cp in first:
        cp.wait()

    lane = lax.broadcasted_iota(jnp.int32, (ROWS, META), 1).astype(F32)
    p_t = prob_v[...]
    p_hi = p_t.astype(BF16).astype(F32)
    terms = jnp.concatenate([ids_v[...].astype(F32), jnp.zeros((8, ROWS), F32), p_hi, p_t - p_hi], axis=0)
    put = (
        lax.broadcasted_iota(jnp.int32, (32, META), 0) == lax.broadcasted_iota(jnp.int32, (32, META), 1)
    ).astype(F32)
    meta = dot(terms.astype(BF16), put.astype(BF16), 0, 0)
    idf = meta[:, 0:8]
    named = jnp.zeros((ROWS, META), F32)
    for k in range(8):
        named = named + (lane == idf[:, k : k + 1]).astype(F32)
    earlier = (
        lax.broadcasted_iota(jnp.int32, (ROWS, ROWS), 1)
        < lax.broadcasted_iota(jnp.int32, (ROWS, ROWS), 0)
    ).astype(F32)
    before = dot(earlier.astype(BF16), named.astype(BF16), 1, 0)
    for k in range(8):
        ek = idf[:, k : k + 1]
        slot = jnp.sum(jnp.where(lane == ek, before, 0.0), axis=1, keepdims=True)
        meta = jnp.where(lane == float(8 + k), slot, meta)
    blocks[0, :, pl.ds(0, META)] = meta.astype(BF16)
    lane_i = lax.broadcasted_iota(jnp.int32, (ROWS, META), 1)
    lane_j = lane_i // SLOTS
    lane_e = ((lane_j // NC) * NZ + z) * NC + lax.rem(lane_j, NC)
    lane_code = (lane_e * SLOTS + lax.rem(lane_i, SLOTS)).astype(F32)

    def matches(m):
        return [
            (m[:, k : k + 1] * float(SLOTS) + m[:, 8 + k : 9 + k]) == lane_code for k in range(8)
        ]

    def picks(m):
        pick = functools.reduce(jnp.logical_or, matches(m))
        return jnp.where(pick, 1.0, 0.0).astype(BF16)

    own_pick = picks(meta)

    def pick(d, mask, p, n):
        rows = dot(mask, blocks[d, :, pl.ds(META + p * SLICE, n * SLICE)], 0, 0).astype(BF16)
        cols = pl.ds(p * SLICE, n * SLICE)
        picked[d, :, :, cols] = rows.reshape(ROW, SLOTS, n * SLICE)
        arrived[d, me, :, cols] = picked[d, me, :, cols]

    def send_row(d, p, n, ss, rs):
        cols = pl.ds(p * SLICE, n * SLICE)
        for i in FAR_FIRST:
            j = other(i)
            send(
                picked.at[d, j, :, cols], arrived.at[d, me, :, cols], ss.at[j], rs.at[me], in_row(j)
            ).start()

    def pass_on(d, cols, ss, rs):
        way = 1 - 2 * (d % 2)
        if d in (5, 6):
            part = pl.ds(32 * (d - 5), 32)
            send(
                blocks.at[d, part, cols], blocks.at[7, part, cols],
                ss.at[d + 2], rs.at[d + 2], along_z(way),
            ).start()
        elif d < 5:
            send(
                blocks.at[d, :, cols], blocks.at[d + 2, :, cols],
                ss.at[d + 2], rs.at[d + 2], along_z(way),
            ).start()

    def block_there(d, cols, rs):
        if d == 7:
            for part in range(2):
                got(blocks.at[7, pl.ds(32 * part, 32), cols], rs.at[7 + part])
        else:
            got(blocks.at[d, :, cols], rs.at[d])

    first_cols = pl.ds(0, FIRST)
    rest_cols = pl.ds(FIRST, REST)

    def mask_of(d):
        return own_pick if d == 0 else picks(blocks[d, :, pl.ds(0, META)].astype(F32))

    def first_step(d):
        if d == 0:
            for way in range(2):
                send(
                    blocks.at[0, :, first_cols], blocks.at[1 + way, :, first_cols],
                    zf_s.at[1 + way], zf_r.at[1 + way], along_z(2 * way - 1),
                ).start()
        else:
            block_there(d, first_cols, zf_r)
            pass_on(d, first_cols, zf_s, zf_r)
            pick(d, mask_of(d), 0, 1)
        send_row(d, 0, 1, xf_s.at[d], xf_r.at[d])

    def gather_step(p):
        got(blocks.at[0, :, place(p)], pg_r.at[p - 1])
        for way in range(2):
            send(
                blocks.at[0, :, place(p)], blocks.at[1 + way, :, place(p)],
                zs_s.at[way, p - 1], zs_r.at[way, p - 1], along_z(2 * way - 1),
            ).start()
        pick(0, own_pick, p, 1)
        send_row(0, p, 1, xs_s.at[p - 1], xs_r.at[p - 1])

    def rest_step(d):
        if d <= 2:
            for p in range(1, 4):
                got(blocks.at[d, :, place(p)], zs_r.at[d - 1, p - 1])
        else:
            block_there(d, rest_cols, z_r)
        pass_on(d, rest_cols, z_s, z_r)

    def block_step(d):
        pick(d, mask_of(d), 1, 3)
        send_row(d, 1, 3, x_s.at[d], x_r.at[d])

    pick(0, own_pick, 0, 1)
    pl.semaphore_wait(barrier, 5 + 7 + 7)

    for p in (3, 1, 2):
        send(
            blocks.at[0, :, place(0)], blocks.at[0, :, place(p)],
            pg_s.at[p - 1], pg_r.at[p - 1], along_y(-PLACES[p]),
        ).start()

    def swap_weights():
        for a, ref in enumerate((gate, up)):
            for p in range(4):
                to = pl.ds(p * SLICE, SLICE)
                send(
                    ref.at[pl.ds(0, PIECE), column(t + NY - 1, p)],
                    weights.at[pl.ds(3 * HID + a * PIECE, PIECE), to],
                    w_s.at[0, a, p], w_r.at[0, a, p], along_y(-1),
                ).start()
                send(
                    ref.at[pl.ds(PIECE, PIECE), column(t + 1, p)],
                    weights.at[pl.ds(2 * HID + a * PIECE, PIECE), to],
                    w_s.at[1, a, p], w_r.at[1, a, p], along_y(1),
                ).start()

    def weights_there():
        for cp in local:
            cp.wait()
        for a in range(2):
            for j in range(4):
                to = pl.ds(j * SLICE, SLICE)
                got(weights.at[pl.ds(3 * HID + a * PIECE, PIECE), to], w_r.at[0, a, j])
                got(weights.at[pl.ds(2 * HID + a * PIECE, PIECE), to], w_r.at[1, a, j])

    def partials(g):
        for i in range(1, ROW):
            src = other(i)
            got(arrived.at[g, src, :, pl.ds(0, SLICE)], xf_r.at[g, src])
            if g == 0:
                for p in range(1, 4):
                    got(arrived.at[0, src, :, pl.ds(p * SLICE, SLICE)], xs_r.at[p - 1, src])
            else:
                got(arrived.at[g, src, :, pl.ds(SLICE, REST)], x_r.at[g, src])
        rows = arrived[g].reshape(GROUP_ROWS, HALF)
        part = dot(weights[pl.ds(2 * HID, 2 * HID)], rows, 1, 1).astype(BF16)
        for side in range(2):
            part_out[g, side] = part[side * HID : (side + 1) * HID]
            send(
                part_out.at[g, side], part_in.at[g, 1 - side],
                p_s.at[g, side], p_r.at[g, 1 - side], along_y(2 * side - 1),
            ).start()
        own[g] = dot(weights[pl.ds(0, 2 * HID)], rows, 1, 1)

    def activate(g):
        for side in range(2):
            got(part_in.at[g, side], p_r.at[g, side])
            lo = pl.ds(side * PIECE, PIECE)
            gv = own[g, lo] + part_in[g, side, pl.ds(0, PIECE)].astype(F32)
            uv = own[g, pl.ds(HID + side * PIECE, PIECE)] + part_in[
                g, side, pl.ds(PIECE, PIECE)
            ].astype(F32)
            hidden[g, t, lo] = (gv / (1.0 + jnp.exp(-gv)) * uv).astype(BF16)
        for way in range(2):
            send(
                hidden.at[g, t], hidden.at[g, t], h_s.at[g, way, 0], h_r.at[g, way, 0],
                along_y(1 - 2 * way),
            ).start()

    def forward(g, h):
        for way in range(2):
            src = lax.rem(t + (h if way else NY - h), NY)
            ref = hidden.at[g, src]
            got(ref, h_r.at[g, way, h - 1])
            if h == 3:
                ref = hidden.at[g, src, pl.ds(way * PIECE, PIECE)]
            send(ref, ref, h_s.at[g, way, h], h_r.at[g, way, h], along_y(1 - 2 * way)).start()

    def project(g):
        far = lax.rem(t + 4, NY)
        for way in range(2):
            got(hidden.at[g, far, pl.ds(way * PIECE, PIECE)], h_r.at[g, way, 3])
        h = hidden[g].reshape(NY * HID, GROUP_ROWS)
        o = dot(h, down_v[...], 0, 0).astype(BF16)
        outputs[g] = o.reshape(ROW, SLOTS, SLICE)
        returned[g, me] = outputs[g, me]
        for i in FAR_FIRST:
            j = other(i)
            send(
                outputs.at[g, j], returned.at[g, me], o_s.at[g, j], o_r.at[g, me], in_row(j)
            ).start()

    def combine(g):
        for i in range(1, ROW):
            src = other(i)
            got(returned.at[g, src], o_r.at[g, src])
        m = blocks[g, :, pl.ds(0, META)].astype(F32)
        hi = jnp.zeros((ROWS, META), F32)
        lo = jnp.zeros((ROWS, META), F32)
        for k, match in enumerate(matches(m)):
            hi = jnp.where(match, m[:, 16 + k : 17 + k], hi)
            lo = jnp.where(match, m[:, 24 + k : 25 + k], lo)
        vals = returned[g].reshape(GROUP_ROWS, SLICE)
        total = dot(hi.astype(BF16), vals, 1, 0) + dot(lo.astype(BF16), vals, 1, 0)
        sums_out[g] = total.astype(BF16)

        if g == 0:
            own_sum[...] = total
        else:
            send(sums_out.at[g], sums_in.at[g], f_s.at[g], f_r.at[g], along_z(offset(g))).start()

    def drain(g):
        for i in range(1, ROW):
            j = other(i)
            sent(picked.at[g, j, :, pl.ds(0, SLICE)], xf_s.at[g, j])
            if g == 0:
                for p in range(1, 4):
                    sent(picked.at[0, j, :, pl.ds(p * SLICE, SLICE)], xs_s.at[p - 1, j])
            else:
                sent(picked.at[g, j, :, pl.ds(SLICE, REST)], x_s.at[g, j])
        for side in range(2):
            sent(part_out.at[g, side], p_s.at[g, side])
            for h in range(3):
                sent(hidden.at[g, 0], h_s.at[g, side, h])
        for side in range(2):
            sent(hidden.at[g, 0, pl.ds(0, PIECE)], h_s.at[g, side, 3])
        for i in range(1, ROW):
            j = other(i)
            sent(outputs.at[g, j], o_s.at[g, j])

    run = {
        "M": first_step, "G": gather_step, "Z": rest_step, "B": block_step, "V": lambda k: swap_weights(), "A": partials, "S": activate, "P": project, "C": combine, "D": drain,
        "1": lambda k: forward(k, 1), "2": lambda k: forward(k, 2), "3": lambda k: forward(k, 3),
        "W": lambda k: weights_there(),
    }
    for step in ORDER:
        run[step[0]](int(step[1]))

    drain(1)
    for i in range(3):
        sent(blocks.at[0, :, place(0)], pg_s.at[i])
    for a in range(2):
        for j in range(4):
            for way in range(2):
                sent(weights.at[pl.ds(0, PIECE), pl.ds(0, SLICE)], w_s.at[way, a, j])
    for way in range(2):
        for p in range(1, 4):
            sent(blocks.at[0, :, place(p)], zs_s.at[way, p - 1])
        sent(blocks.at[0, :, first_cols], zf_s.at[1 + way])
    for d in range(3, 7):
        sent(blocks.at[d, :, first_cols], zf_s.at[d])
        sent(blocks.at[d, :, rest_cols], z_s.at[d])
    for d in (7, 8):
        sent(blocks.at[7, pl.ds(0, 32), first_cols], zf_s.at[d])
        sent(blocks.at[7, pl.ds(0, 32), rest_cols], z_s.at[d])

    total = own_sum[...]
    for d in (2, 3, 4, 5, 6, 7, 1):
        got(sums_in.at[d], f_r.at[d])
        total = total + sums_in[d].astype(F32)
    out[...] = total.astype(BF16)
    for d in range(1, NZ):
        sent(sums_out.at[d], f_s.at[d])


def local(tokens, gate_weight, up_weight, down_weight, expert_ids, gate_probs):
    hbm = pl.BlockSpec(memory_space=pltpu.HBM)
    vmem = pl.BlockSpec(memory_space=pltpu.VMEM)
    dma = pltpu.SemaphoreType.DMA
    scratch = [
        pltpu.VMEM((NZ, ROWS, HALF + META), BF16),
        pltpu.VMEM((NZ, ROW, SLOTS, HALF), BF16),
        pltpu.VMEM((NZ, ROW, SLOTS, HALF), BF16),
        pltpu.VMEM((4 * HID, HALF), BF16),
        pltpu.VMEM((NY * HID, SLICE), BF16),
        pltpu.VMEM((NZ, 2 * HID, GROUP_ROWS), F32),
        pltpu.VMEM((NZ, 2, HID, GROUP_ROWS), BF16),
        pltpu.VMEM((NZ, 2, HID, GROUP_ROWS), BF16),
        pltpu.VMEM((NZ, NY, HID, GROUP_ROWS), BF16),
        pltpu.VMEM((NZ, ROW, SLOTS, SLICE), BF16),
        pltpu.VMEM((NZ, ROW, SLOTS, SLICE), BF16),
        pltpu.VMEM((NZ, ROWS, SLICE), BF16),
        pltpu.VMEM((NZ, ROWS, SLICE), BF16),
        pltpu.VMEM((ROWS, SLICE), F32),
        pltpu.VMEM((8, ROWS), jnp.int32),
        pltpu.VMEM((8, ROWS), F32),
        dma((3,)),
        dma((3,)), dma((3,)),
        dma((2, 2, 4)), dma((2, 2, 4)), dma((2, 4)), dma((1,)),
        dma((2, 3)), dma((2, 3)), dma((9,)), dma((9,)), dma((9,)), dma((9,)),
        dma((3, ROW)), dma((3, ROW)), dma((NZ, ROW)), dma((NZ, ROW)), dma((NZ, ROW)), dma((NZ, ROW)),
        dma((NZ, 2)), dma((NZ, 2)),
        dma((NZ, 2, 4)), dma((NZ, 2, 4)),
        dma((NZ, ROW)), dma((NZ, ROW)),
        dma((NZ,)), dma((NZ,)),
    ]
    return pl.pallas_call(
        kernel,
        out_shape=jax.ShapeDtypeStruct((ROWS, SLICE), BF16),
        in_specs=[hbm] * 6,
        out_specs=vmem,
        scratch_shapes=scratch,
        compiler_params=pltpu.CompilerParams(
            collective_id=0, has_side_effects=True, vmem_limit_bytes=(64 << 20) - (1 << 18)
        ),
        cost_estimate=pl.CostEstimate(flops=5_000_000_000, bytes_accessed=5_000_000, transcendentals=200_000),
    )(tokens, gate_weight[0], up_weight[0], down_weight[0], expert_ids.T, gate_probs.T)


def solution(mesh):
    in_specs = (
        P("expert", "tensor"),
        P("expert", "tensor", None),
        P("expert", "tensor", None),
        P("expert", None, "tensor"),
        P("expert", None),
        P("expert", None),
    )
    out_specs = P("expert", "tensor")
    return jax.shard_map(local, mesh=mesh, in_specs=in_specs, out_specs=out_specs, check_vma=False)
```
